512 devices in a mesh: rows: 128 (over z, y, core), rep: 4 (over x).
Axes of the slice: x: 4, y: 8, z: 8, core: 2. Of those that a mesh axis runs over, the one named last changes fastest.
Arguments:
- event_slots: int32 [512, 128], P(('rows', 'rep')), may hold values from 0 to 383, as said below
- fetch_rows: int32 [512, 256], P(('rows', 'rep')), may hold values from 0 to 255, as said below
- fetch_counts: int32 [512, 128], P(('rows', 'rep')), may hold values from 1 to 2, as said below
- hot_table: float32 [128, 512], replicated, may hold values from -6 to 6
- hot_accum: float32 [128], replicated, may hold values from 0.05 to 2
- cold_table: float32 [32768, 512], P('rows'), may hold values from -6 to 6
- cold_accum: float32 [32768], P('rows'), may hold values from 0.05 to 2
- ln_gain: float32 [512], replicated, may hold values from 0.1 to 1.9
- ln_bias: float32 [512], replicated, may hold values from -3 to 3
- w_in: bfloat16 [512, 2048], replicated, may hold values from -0.25 to 0.25
- w_out: bfloat16 [512, 512], replicated, may hold values from -0.25 to 0.25
- out_grad: bfloat16 [65536, 512], P(('rows', 'rep')), may hold values from -6 to 6
Outputs:
- new_hot_table: float32 [128, 512], replicated
- new_hot_accum: float32 [128], replicated
- new_cold_table: float32 [32768, 512], P('rows')
- new_cold_accum: float32 [32768], P('rows')
The draws below stay inside these ranges and needn't reach their ends.
Inputs may be any that keep to these rules, and one draw needn't show every extreme that they name: `event_slots`: rows of the lookup buffer: the 128 hot rows, then 2 slots for each of the 128 owners; an event names slot k of owner j only if k is below that device's fetch_counts for j. `fetch_rows`: rows local to the owner's shard, distinct within one owner's 2 slots of one device; slots at or past the count are padding. `fetch_counts`: some owner is asked for 2 rows by every device.
All inputs are finite; a program needn't handle non-finite values.
Results may differ from the reference program's by a relative error of at most 0.0065.
Values sent between devices are 32-bit elements; how exact they have to be, the bound alone decides.
A program may use at most 64 MiB of HBM per device.

```python
import math
import jax
import jax.numpy as jnp
from jax import lax

D = 512
HEADS = 4
HEAD = 128
SEQ_LEN = 128
ROWS_DEV = 256
HOT_ROWS = 128
SLOT = 2
TOKENS = 65536
COLD_ROWS = 32768
N_ROWS = 128
DEVICES = 512


def owner_counts(key):
    base = jax.random.fold_in(key, 11)
    counts = jax.random.randint(jax.random.fold_in(base, 1), (DEVICES, N_ROWS), 1, SLOT + 1)
    full_owner = jax.random.randint(jax.random.fold_in(base, 2), (), 0, N_ROWS)
    column = jnp.arange(N_ROWS, dtype=jnp.int32)[None, :] == full_owner
    return jnp.where(column, SLOT, counts).astype(jnp.int32)


def draw_fetch_counts(key, part):
    return owner_counts(key)


def draw_fetch_rows(key, part):
    stride = ROWS_DEV // SLOT
    offsets = jax.random.randint(jax.random.fold_in(key, 23), (DEVICES, N_ROWS, SLOT), 0, stride)
    picked = offsets + jnp.arange(SLOT, dtype=jnp.int32)[None, None, :] * stride
    return picked.reshape(DEVICES, N_ROWS * SLOT).astype(jnp.int32)


def draw_event_slots(key, part):
    counts = owner_counts(key)
    shape = (DEVICES, SEQ_LEN)
    hot_pick = jax.random.randint(jax.random.fold_in(key, 31), shape, 0, HOT_ROWS)
    owner = jax.random.randint(jax.random.fold_in(key, 32), shape, 0, N_ROWS)
    limit = jnp.take_along_axis(counts, owner, axis=1)
    within = jax.random.randint(jax.random.fold_in(key, 33), shape, 0, limit)
    cold_pick = HOT_ROWS + owner * SLOT + within
    coin = jax.random.randint(jax.random.fold_in(key, 34), shape, 0, 2)
    return jnp.where(coin == 0, hot_pick, cold_pick).astype(jnp.int32)


def levels(own_key, shape, cuts, low, high):
    def one(dim, blocks):
        steps = jax.random.uniform(jax.random.fold_in(jax.random.fold_in(own_key, 6), dim), (blocks,), jnp.float32, low / len(cuts), high / len(cuts))
        return jnp.repeat(jnp.exp(steps), shape[dim] // blocks).reshape((-1,) + (1,) * (len(shape) - dim - 1))

    loudness = one(*cuts[0])
    for cut in cuts[1:]:
        loudness = loudness * one(*cut)
    return loudness


def gaussian(rng, shape, width, reach, cuts=(), held_as=jnp.bfloat16):
    values = width * jax.random.normal(rng, shape, jnp.float32)
    if cuts:
        values = values * levels(rng, shape, cuts, -0.22, 0.18)
    return jnp.clip(values, -reach, reach).astype(held_as)


def setup_inputs(seed: int = 0) -> dict:
    key_list = jax.random.split(jax.random.key(seed), 13)
    return {
        "event_slots": draw_event_slots(jax.random.fold_in(key_list[12], 71), 0),
        "fetch_rows": draw_fetch_rows(jax.random.fold_in(key_list[12], 71), 0),
        "fetch_counts": draw_fetch_counts(jax.random.fold_in(key_list[12], 71), 0),
        "hot_table": gaussian(key_list[3], (HOT_ROWS, D), 1.0, 6.0, (), jnp.float32),
        "hot_accum": jnp.clip(jnp.exp(jax.random.uniform(key_list[4], (HOT_ROWS,), jnp.float32, math.log(0.05), math.log(2.0))), 0.05, 2.0),
        "cold_table": gaussian(key_list[5], (COLD_ROWS, D), 1.0, 6.0, ((0, 128),), jnp.float32),
        "cold_accum": jnp.clip(jnp.exp(math.log(2.0) - 3.6888794 * jax.random.uniform(key_list[6], (COLD_ROWS,), jnp.float32) ** levels(key_list[6], (COLD_ROWS,), ((0, 128),), -0.2, 0.2)), 0.05, 2.0),
        "ln_gain": jnp.clip(1.0 + 0.18 * jax.random.normal(key_list[7], (D,), jnp.float32), 0.1, 1.9),
        "ln_bias": gaussian(key_list[8], (D,), 0.5, 3.0, (), jnp.float32),
        "w_in": gaussian(key_list[9], (D, 4 * HEADS * HEAD), D ** -0.5, 0.25),
        "w_out": gaussian(key_list[10], (HEADS * HEAD, D), (HEADS * HEAD) ** -0.5, 0.25),
        "out_grad": gaussian(key_list[11], (TOKENS, D), 1.0, 6.0, ((0, 512),)),
    }


STEP_RATE = 0.5

def hstu_layer(looked_up, ln_gain, ln_bias, w_in, w_out):
    seq_rows = looked_up.shape[0]
    inner = w_out.shape[0]
    n_heads = inner // HEAD
    row_mean = lax.optimization_barrier(jnp.mean(looked_up, axis=1, keepdims=True))
    centered = looked_up - row_mean
    row_var = lax.optimization_barrier(jnp.mean(centered * centered, axis=1, keepdims=True))
    normed = (centered * lax.rsqrt(row_var + 1e-05) * ln_gain + ln_bias).astype(jnp.bfloat16)
    projected = jax.nn.silu(jnp.dot(normed, w_in, preferred_element_type=jnp.float32)).astype(jnp.bfloat16)
    gates_u, values_v, queries, keys_k = jnp.split(projected, 4, axis=1)
    head_shape = (seq_rows, n_heads, HEAD)
    scores = jnp.einsum('qhd,khd->hqk', queries.reshape(head_shape).astype(jnp.float32), keys_k.reshape(head_shape).astype(jnp.float32)) * HEAD ** (-0.5)
    causal = (lax.broadcasted_iota(jnp.int32, (seq_rows, seq_rows), 0) >= lax.broadcasted_iota(jnp.int32, (seq_rows, seq_rows), 1)).astype(jnp.float32)
    attention = (jax.nn.silu(scores) * causal * (1.0 / seq_rows)).astype(jnp.bfloat16)
    mixed_val = jnp.einsum('hqk,khd->qhd', attention.astype(jnp.float32), values_v.reshape(head_shape).astype(jnp.float32)).reshape(seq_rows, inner)
    mixed_mean = lax.optimization_barrier(jnp.mean(mixed_val, axis=1, keepdims=True))
    mixed_cent = mixed_val - mixed_mean
    mixed_var = lax.optimization_barrier(jnp.mean(mixed_cent * mixed_cent, axis=1, keepdims=True))
    gated_val = (mixed_cent * lax.rsqrt(mixed_var + 1e-06) * gates_u.astype(jnp.float32)).astype(jnp.bfloat16)
    layer_out = looked_up + jnp.dot(gated_val, w_out, preferred_element_type=jnp.float32)
    return layer_out.astype(jnp.bfloat16)

def adagrad(table_rows, accum_rows, grad_rows):
    new_accum = accum_rows + lax.optimization_barrier(jnp.mean(grad_rows * grad_rows, axis=1))
    return (table_rows - STEP_RATE * grad_rows * lax.rsqrt(new_accum)[:, None], new_accum)

def reference(event_slots, fetch_rows, fetch_counts, hot_table, hot_accum, cold_table, cold_accum, ln_gain, ln_bias, w_in, w_out, out_grad):
    device_count = event_slots.shape[0]
    seq_rows = event_slots.shape[1]
    feature_width = hot_table.shape[1]
    hot_rows = hot_table.shape[0]
    per_owner = fetch_rows.shape[1] // N_ROWS
    rows_shard = cold_table.shape[0] // N_ROWS
    owner_base = (jnp.arange(N_ROWS, dtype=jnp.int32) * rows_shard)[:, None]
    cotangents = out_grad.reshape(device_count, seq_rows, feature_width)

    def forward_for(ln_g, ln_b):

        def forward(looked_up):
            return hstu_layer(looked_up, ln_g, ln_b, w_in, w_out)
        return forward
    forward = forward_for(ln_gain, ln_bias)

    def one_device(running, inputs):
        hot_sum, cold_sum = running
        event_rows, wanted, counts, cotangent = inputs
        global_rows = (wanted.reshape(N_ROWS, per_owner) + owner_base).reshape(-1).astype(jnp.int32)
        live_mask = (jnp.arange(per_owner, dtype=jnp.int32)[None, :] < counts[:, None]).reshape(-1, 1).astype(jnp.float32)
        fetched = cold_table[global_rows] * live_mask
        buffer = jnp.concatenate([hot_table, fetched], axis=0)
        looked_up = buffer[event_rows]
        _, backward = jax.vjp(forward, looked_up)
        d_lookup, = backward(cotangent)
        buffer_grad = jax.ops.segment_sum(d_lookup, event_rows, num_segments=hot_rows + N_ROWS * per_owner)
        hot_sum = hot_sum + buffer_grad[:hot_rows]
        cold_sum = cold_sum.at[global_rows].add(buffer_grad[hot_rows:] * live_mask)
        return ((hot_sum, cold_sum), None)
    start = (jnp.zeros(hot_table.shape, jnp.float32), jnp.zeros(cold_table.shape, jnp.float32))
    (hot_grad, cold_grad), _ = lax.scan(one_device, start, (event_slots, fetch_rows, fetch_counts, cotangents))
    new_hot_table, new_hot_accum = adagrad(hot_table, hot_accum, hot_grad)
    new_cold_table, new_cold_accum = adagrad(cold_table, cold_accum, cold_grad)
    return (new_hot_table, new_hot_accum, new_cold_table, new_cold_accum)
```

```python
import functools

import jax
import jax.numpy as jnp
from jax import lax
from jax.experimental import pallas as pl
from jax.experimental.pallas import tpu as pltpu
from jax.sharding import Mesh
from jax.sharding import PartitionSpec as P

HEAD = 128
STEP_RATE = 0.5
NZ, NY, NC, NX = 8, 8, 2, 4
NYC = NY * NC
OWNERS = NZ * NYC
ALL = ("z", "y", "c", "x")
BY_ROWS = ("z", "y", "c")
MESH = pl.DeviceIdType.MESH
F32, BF16 = jnp.float32, jnp.bfloat16


def dot(a, b, dims=((1,), (0,))):
    return lax.dot_general(a, b, (dims, ((), ())), preferred_element_type=F32)


def two_parts(value):
    high = value.astype(BF16)
    low = (value - high.astype(F32)).astype(BF16)
    return high, low


def picked(onehot, value, dims=((1,), (0,))):
    high, low = two_parts(value)
    return dot(onehot, high, dims) + dot(onehot, low, dims)


def sigmoid(x):
    return 0.5 * jnp.tanh(0.5 * x) + 0.5


def iota(shape, dim):
    return lax.broadcasted_iota(jnp.int32, shape, dim)


def layer_gradient(looked_up, gain, bias, w_in_ref, w_out_ref, out_grad):
    seq, width = looked_up.shape
    inner = w_out_ref.shape[0]
    mean = jnp.mean(looked_up, axis=1, keepdims=True)
    centered = looked_up - mean
    inv = lax.rsqrt(jnp.mean(centered * centered, axis=1, keepdims=True) + 1e-05)
    xhat = centered * inv
    normed = (xhat * gain + bias).astype(BF16)
    parts, slopes = [], []
    for b in range(4):
        pre = dot(normed, w_in_ref[:, b * inner : (b + 1) * inner])
        sig = sigmoid(pre)
        act = pre * sig
        parts.append(act.astype(BF16))
        slopes.append(sig + act * (1.0 - sig))
    gates, values, queries, keys = parts
    causal = iota((seq, seq), 0) >= iota((seq, seq), 1)
    scale = HEAD ** (-0.5)
    heads = [slice(h * HEAD, (h + 1) * HEAD) for h in range(inner // HEAD)]
    attention, slope_att, mixed = [], [], []
    for h in heads:
        scores = dot(queries[:, h], keys[:, h], ((1,), (1,))) * scale
        sig = sigmoid(scores)
        act = scores * sig
        att = jnp.where(causal, act * (1.0 / seq), 0.0).astype(BF16)
        attention.append(att)
        slope_att.append(jnp.where(causal, (sig + act * (1.0 - sig)) * (scale / seq), 0.0))
        mixed.append(dot(att, values[:, h]))
    mixed = jnp.concatenate(mixed, axis=1)
    mixed = mixed - jnp.mean(mixed, axis=1, keepdims=True)
    inv2 = lax.rsqrt(jnp.mean(mixed * mixed, axis=1, keepdims=True) + 1e-06)
    mhat = mixed * inv2
    d_gated = dot(out_grad, w_out_ref[...], ((1,), (1,))).astype(BF16).astype(F32)
    d_gates = (d_gated * mhat).astype(BF16)
    d_mhat = d_gated * gates.astype(F32)
    d_mixed = inv2 * (
        d_mhat
        - jnp.mean(d_mhat, axis=1, keepdims=True)
        - mhat * jnp.mean(d_mhat * mhat, axis=1, keepdims=True)
    )
    d_mixed = d_mixed.astype(BF16)
    d_values, d_queries, d_keys = [], [], []
    for n, h in enumerate(heads):
        d_att = dot(d_mixed[:, h], values[:, h], ((1,), (1,))).astype(BF16).astype(F32)
        d_values.append(dot(attention[n], d_mixed[:, h], ((0,), (0,))).astype(BF16))
        d_raw = (d_att * slope_att[n]).astype(BF16)
        d_queries.append(dot(d_raw, keys[:, h]).astype(BF16))
        d_keys.append(dot(d_raw, queries[:, h], ((0,), (0,))).astype(BF16))
    d_parts = [
        d_gates,
        jnp.concatenate(d_values, axis=1),
        jnp.concatenate(d_queries, axis=1),
        jnp.concatenate(d_keys, axis=1),
    ]
    d_normed = jnp.zeros((seq, width), F32)
    for b in range(4):
        d_pre = (d_parts[b].astype(F32) * slopes[b]).astype(BF16)
        d_normed = d_normed + dot(d_pre, w_in_ref[:, b * inner : (b + 1) * inner], ((1,), (1,)))
    d_xhat = d_normed.astype(BF16).astype(F32) * gain
    return out_grad.astype(F32) + inv * (
        d_xhat
        - jnp.mean(d_xhat, axis=1, keepdims=True)
        - xhat * jnp.mean(d_xhat * xhat, axis=1, keepdims=True)
    )


def step_kernel(
    slots_ref,
    rows_ref,
    counts_ref,
    hot_ref,
    table_ref,
    gain_ref,
    bias_ref,
    w_in_ref,
    w_out_ref,
    out_grad_ref,
    cold_out,
    hot_out,
    idx_z,
    idx_n,
    idx_all,
    idx_x,
    send_a,
    recv_a,
    x_send,
    x_recv,
    send_b,
    recv_b,
    hot_c,
    hot_cr,
    hot_z,
    hot_zr,
    hot_t,
    hot_yr,
    hot_g,
    hot_f,
    sems,
    z_s,
    z_r,
    yc_s,
    yc_r,
    xi_s,
    xi_r,
    xh_s,
    xh_r,
    xc_s,
    xc_r,
    hz_s,
    hz_r,
    hy_s,
    hy_r,
    hg_s,
    hg_r,
    xo_s,
    xo_r,
    xp_s,
    xp_r,
):
    z, y, c, x = (lax.axis_index(a) for a in ALL)
    yc = y * NC + c
    me = yc * NZ + z
    width = hot_ref.shape[1]
    lanes = width // NX

    def along(axis, o):
        if axis == "z":
            t = lax.rem(z + o, NZ)
            return t, (t, y, c, x)
        if axis == "y":
            t = lax.rem(y + o, NY)
            return t, (z, t, c, x)
        if axis == "yc":
            t = lax.rem(yc + o, NYC)
            return t, (z, lax.div(t, NC), lax.rem(t, NC), x)
        t = lax.rem(x + o, NX)
        return t, (z, y, c, t)

    SIZE = {"z": NZ, "y": NY, "yc": NYC, "x": NX}

    def exchange(axis, src, dst, s, r):
        copies = []
        for o in range(1, SIZE[axis]):
            t, dev = along(axis, o)
            copies.append(
                pltpu.make_async_remote_copy(
                    src_ref=src(t),
                    dst_ref=dst,
                    send_sem=s.at[o],
                    recv_sem=r.at[o],
                    device_id=dev,
                    device_id_type=MESH,
                )
            )
        for cp in copies:
            cp.start()
        return copies

    def to_sibling(src, dst, n):
        cp = pltpu.make_async_remote_copy(
            src_ref=src,
            dst_ref=dst,
            send_sem=sems.at[n],
            recv_sem=sems.at[n + 1],
            device_id=(z, y, 1 - c, x),
            device_id_type=MESH,
        )
        cp.start()
        return cp

    def arrived(copies):
        for cp in copies:
            cp.wait_recv()

    def tile(q):
        return pl.ds(pl.multiple_of(q * 8, 8), 8)

    def scatter_tiles(src, dst, n):
        @pl.loop(1, OWNERS)
        def _(o):
            p = lax.rem(o * 37, OWNERS)
            tz = lax.rem(z + lax.rem(p, NZ), NZ)
            ty = lax.rem(y + lax.rem(lax.div(p, NZ), NY), NY)
            tc = lax.rem(c + lax.div(p, NZ * NY), NC)
            q = (ty * NC + tc) * NZ + tz
            pltpu.make_async_remote_copy(
                src_ref=src.at[tile(q)],
                dst_ref=dst.at[tile(me)],
                send_sem=sems.at[n],
                recv_sem=sems.at[n + 1],
                device_id=(tz, ty, tc, x),
                device_id_type=MESH,
            ).start()

    def tiles_wait(ref, n):
        whole = ref.at[pl.ds(0, (OWNERS - 1) * 8)]
        pltpu.make_async_copy(whole, whole, sems.at[n]).wait()

    barrier = pltpu.get_barrier_semaphore()
    greeted = 0
    for axis in ("z", "yc", "x"):
        for o in range(1, SIZE[axis]):
            pl.semaphore_signal(barrier, inc=1, device_id=along(axis, o)[1], device_id_type=MESH)
            greeted += 1
    pl.semaphore_wait(barrier, greeted)

    pending = exchange("z", lambda t: rows_ref, idx_z.at[z], z_s, z_r)
    idx_z[z] = rows_ref[...]
    table_high, table_low = two_parts(table_ref[...])
    arrived(pending)
    every = jnp.concatenate([idx_z[i] for i in range(NZ)], axis=0).astype(F32)
    mine = pltpu.roll(every, lax.rem(8 * 32 - 32 * z, 256), axis=1)[:, :128]
    idx_n[...] = mine
    more = exchange("yc", lambda t: idx_n, idx_all.at[yc], yc_s, yc_r)
    idx_all[yc] = mine
    pending += more
    arrived(more)
    asked = idx_all[...].reshape(OWNERS, 128)
    lane = iota((OWNERS, 128), 1)
    line = iota((OWNERS, table_ref.shape[0]), 1).astype(F32)
    columns = []
    for k in range(2):
        column = jnp.sum(jnp.where(lane == 2 * yc + k, asked, 0.0), axis=1, keepdims=True)
        columns.append(column)
        onehot = (column == line).astype(BF16)
        found = dot(onehot, table_high) + dot(onehot, table_low)
        for i in range(NX):
            send_a[pl.ds(k * NX + i, OWNERS, stride=8), :] = found[:, i * lanes : (i + 1) * lanes]
    scatter_tiles(send_a, recv_a, 0)
    recv_a[tile(me), :] = send_a[tile(me), :]

    both = jnp.where(lane == 0, columns[0], jnp.where(lane == 1, columns[1], 0.0))
    idx_n2 = jnp.transpose(both)[:8, :]
    idx_x[x] = idx_n2
    more = exchange("x", lambda t: idx_x.at[x], idx_x.at[x], xi_s, xi_r)
    pending += more

    owner_of = lambda q: lax.rem(q, NZ) * NYC + lax.div(q, NZ)
    slot_of = jnp.transpose(jnp.broadcast_to(slots_ref[...].astype(F32), (128, 128)))
    lane1 = iota((128, 128), 1)
    order = (iota((128, 128), 0) == owner_of(lane1)).astype(BF16)
    live = dot(jnp.broadcast_to(counts_ref[...].astype(F32), (8, 128)).astype(BF16), order)[:1, :]
    hot_rows = hot_ref.shape[0]
    pick_hot = (slot_of == lane1.astype(F32)).astype(BF16)
    picks = []
    for k in range(2):
        name = (hot_rows + 2 * owner_of(lane1) + k).astype(F32)
        picks.append(((slot_of == name) & (live > k)).astype(BF16))
    looked_hot = picked(pick_hot, hot_ref[...])

    tiles_wait(recv_a, 1)
    looked = []
    for i in range(NX):
        part = looked_hot[:, i * lanes : (i + 1) * lanes]
        for k in range(2):
            part = part + picked(picks[k], recv_a[pl.ds(k * NX + i, OWNERS, stride=8), :])
        looked.append(part)
    looked_up = jnp.concatenate(looked, axis=1)

    d_lookup = layer_gradient(
        looked_up, gain_ref[...], bias_ref[...], w_in_ref, w_out_ref, out_grad_ref[...]
    )

    high, low = two_parts(d_lookup)
    for b, pick in enumerate([pick_hot] + picks):
        total = dot(pick, high, ((0,), (0,))) + dot(pick, low, ((0,), (0,)))
        for i in range(NX):
            x_send[i, b * 128 : (b + 1) * 128, :] = total[:, i * lanes : (i + 1) * lanes]
    hot_part, cold_part = pl.ds(0, 128), pl.ds(128, 256)
    hot_x = exchange("x", lambda t: x_send.at[t, hot_part], x_recv.at[x, hot_part], xh_s, xh_r)
    cold_x = exchange("x", lambda t: x_send.at[t, cold_part], x_recv.at[x, cold_part], xc_s, xc_r)
    pending += hot_x + cold_x
    x_recv[x] = x_send[x]

    arrived(hot_x)
    hot = x_recv[0, :128] + x_recv[1, :128] + x_recv[2, :128] + x_recv[3, :128]
    hot_c[...] = hot.reshape(2, 64, 128)
    swap = to_sibling(hot_c.at[1 - c], hot_cr, 4)
    arrived(cold_x)
    for p in range(NX):
        for k in range(2):
            send_b[pl.ds(p * 2 + k, OWNERS, stride=8), :] = x_recv[
                p, 128 + k * 128 : 256 + k * 128, :
            ]
    swap.wait()
    hot_z[...] = (hot_c[c] + hot_cr[...]).reshape(NZ, 8, 128)
    hot_zs = exchange("z", lambda t: hot_z.at[t], hot_zr.at[z], hz_s, hz_r)
    hot_zr[z] = hot_z[z]
    pending += hot_zs
    scatter_tiles(send_b, recv_b, 2)
    recv_b[tile(me), :] = send_b[tile(me), :]
    arrived(hot_zs)
    hot_t[0] = jnp.sum(hot_zr[...], axis=0)
    hot_ys = exchange("y", lambda t: hot_t.at[0], hot_yr.at[y], hy_s, hy_r)
    hot_yr[y] = hot_t[0]
    pending += hot_ys
    arrived(hot_ys)
    hot_t[1] = jnp.sum(hot_yr[...], axis=0)
    hot_gs = exchange("z", lambda t: hot_t.at[1], hot_g.at[z], hg_s, hg_r)
    hot_g[z] = hot_t[1]
    pending += hot_gs
    arrived(hot_gs)
    hot_f[c] = hot_g[...].reshape(64, 128)
    swap = to_sibling(hot_f.at[c], hot_f.at[c], 6)
    swap.wait()
    hot_out[x] = hot_f[...].reshape(128, 128)
    hot_os = exchange("x", lambda t: hot_out.at[x], hot_out.at[x], xo_s, xo_r)
    pending += hot_os

    arrived(pending[2 * 0 + (NZ - 1) + (NYC - 1) : (NZ - 1) + (NYC - 1) + (NX - 1)])
    tall = iota((table_ref.shape[0], OWNERS), 0).astype(F32)
    sums = [
        (tall == idx_x[p, k : k + 1, :]).astype(BF16) for p in range(NX) for k in range(2)
    ]
    tiles_wait(recv_b, 3)
    grad = jnp.zeros((table_ref.shape[0], 128), F32)
    for n in range(8):
        grad = grad + picked(sums[n], recv_b[pl.ds(n, OWNERS, stride=8), :])
    cold_out[x] = grad
    cold_os = exchange("x", lambda t: cold_out.at[x], cold_out.at[x], xp_s, xp_r)
    pending += cold_os
    arrived(hot_os)
    arrived(cold_os)
    for cp in pending:
        cp.wait_send()
    tiles_wait(recv_a, 0)
    tiles_wait(recv_b, 2)


def step(slots, rows, counts, hot_table, cold_table, gain, bias, w_in, w_out, out_grad):
    vm = pl.BlockSpec(memory_space=pltpu.VMEM)
    dma = pltpu.SemaphoreType.DMA
    cold_rows, width = cold_table.shape
    f32 = lambda *s: pltpu.VMEM(s, F32)
    two = lambda n: [dma((n,)), dma((n,))]
    return pl.pallas_call(
        step_kernel,
        out_shape=(
            jax.ShapeDtypeStruct((NX, cold_rows, width // NX), F32),
            jax.ShapeDtypeStruct((NX, hot_table.shape[0], width // NX), F32),
        ),
        in_specs=[vm] * 10,
        out_specs=(vm, vm),
        scratch_shapes=[
            pltpu.VMEM((NZ, 1, 256), jnp.int32),
            f32(8, 128),
            f32(NYC, 8, 128),
            f32(NX, 8, 128),
            f32(OWNERS * 8, 128),
            f32(OWNERS * 8, 128),
            f32(NX, 384, 128),
            f32(NX, 384, 128),
            f32(OWNERS * 8, 128),
            f32(OWNERS * 8, 128),
            f32(2, 64, 128),
            f32(64, 128),
            f32(NZ, 8, 128),
            f32(NZ, 8, 128),
            f32(2, 8, 128),
            f32(NY, 8, 128),
            f32(NZ, 8, 128),
            f32(2, 64, 128),
            dma((8,)),
            *two(NZ),
            *two(NYC),
            *two(NX),
            *two(NX),
            *two(NX),
            *two(NZ),
            *two(NY),
            *two(NZ),
            *two(NX),
            *two(NX),
        ],
        compiler_params=pltpu.CompilerParams(
            collective_id=0, has_side_effects=True, vmem_limit_bytes=48 << 20
        ),
        cost_estimate=pl.CostEstimate(
            flops=1_500_000_000, bytes_accessed=6_000_000, transcendentals=400_000
        ),
        name="step",
    )(slots, rows, counts, hot_table, cold_table, gain, bias, w_in, w_out, out_grad)


def update(grad_ref, table_ref, accum_ref, new_table, new_accum):
    rows = table_ref.shape[0]
    lanes = grad_ref.shape[2]
    total = sum(grad_ref[i] * grad_ref[i] for i in range(NX))
    mean = jnp.sum(total, axis=1, keepdims=True) * (1.0 / table_ref.shape[1])
    for b in range(rows // 128):
        at = slice(b * 128, (b + 1) * 128)
        old = jnp.transpose(jnp.broadcast_to(accum_ref[:, at], (128, 128)))
        new = old + mean[at, :]
        new_accum[:, at] = jnp.transpose(new)[:1, :]
        rate = STEP_RATE * lax.rsqrt(new)
        for i in range(NX):
            col = slice(i * lanes, (i + 1) * lanes)
            new_table[at, col] = table_ref[at, col] - grad_ref[i, at, :] * rate


def adagrad_kernel(
    cold_ref, hot_ref, cold_table, cold_accum, hot_table, hot_accum, o_hot, o_hacc, o_cold, o_cacc
):
    update(hot_ref, hot_table, hot_accum, o_hot, o_hacc)
    update(cold_ref, cold_table, cold_accum, o_cold, o_cacc)


def adagrad(cold_grad, hot_grad, cold_table, cold_accum, hot_table, hot_accum):
    vm = pl.BlockSpec(memory_space=pltpu.VMEM)
    cold_accum, hot_accum = cold_accum.reshape(1, -1), hot_accum.reshape(1, -1)
    out = pl.pallas_call(
        adagrad_kernel,
        out_shape=tuple(
            jax.ShapeDtypeStruct(a.shape, F32)
            for a in (hot_table, hot_accum, cold_table, cold_accum)
        ),
        in_specs=[vm] * 6,
        out_specs=(vm,) * 4,
        compiler_params=pltpu.CompilerParams(vmem_limit_bytes=16 << 20),
        name="adagrad",
    )(cold_grad, hot_grad, cold_table, cold_accum, hot_table, hot_accum)
    return out[0], out[1].reshape(-1), out[2], out[3].reshape(-1)


def on_device(
    event_slots,
    fetch_rows,
    fetch_counts,
    hot_table,
    hot_accum,
    cold_table,
    cold_accum,
    ln_gain,
    ln_bias,
    w_in,
    w_out,
    out_grad,
):
    cold_grad, hot_grad = step(
        event_slots,
        fetch_rows,
        fetch_counts,
        hot_table,
        cold_table,
        ln_gain.reshape(1, -1),
        ln_bias.reshape(1, -1),
        w_in,
        w_out,
        out_grad,
    )
    return adagrad(cold_grad, hot_grad, cold_table, cold_accum, hot_table, hot_accum)


def solution(mesh):
    finer = Mesh(mesh.devices.reshape(NZ, NY, NC, NX), ALL)
    return jax.shard_map(
        on_device,
        mesh=finer,
        in_specs=(
            P(ALL, None),
            P(ALL, None),
            P(ALL, None),
            P(),
            P(),
            P(BY_ROWS, None),
            P(BY_ROWS),
            P(),
            P(),
            P(),
            P(),
            P(ALL, None),
        ),
        out_specs=(P(), P(), P(BY_ROWS, None), P(BY_ROWS)),
        check_vma=False,
    )
```

```python
import functools

import jax
import jax.numpy as jnp
import numpy as np
from jax import lax
from jax.experimental import pallas as pl
from jax.experimental.pallas import tpu as pltpu
from jax.sharding import Mesh
from jax.sharding import PartitionSpec as P

HEAD = 128
STEP_RATE = 0.5
NZ, NY, NC, NX = 8, 8, 2, 4
NYC = NY * NC
OWNERS = NZ * NYC
INPUTS = 11
GROUPS = 4
SPAN = OWNERS // GROUPS


def hops(offset, size):
    return min(offset, size - offset)


def farthest_first():
    offsets = [(a, b, k) for a in range(NZ) for b in range(NY) for k in range(NC)]
    mixed = [offsets[n * 37 % OWNERS] for n in range(OWNERS)]
    far = lambda o: max(hops(o[0], NZ), hops(o[1], NY))
    both = lambda o: hops(o[0], NZ) + hops(o[1], NY)
    return sorted(mixed, key=lambda o: (-far(o), -both(o), o == (0, 0, 0)))


OFFSETS = farthest_first()
ALL = ("z", "y", "c", "x")
BY_ROWS = ("z", "y", "c")
MESH = pl.DeviceIdType.MESH
F32, BF16 = jnp.float32, jnp.bfloat16


def dot(a, b, dims=((1,), (0,))):
    return lax.dot_general(a, b, (dims, ((), ())), preferred_element_type=F32)


def two_parts(value):
    high = value.astype(BF16)
    low = (value - high.astype(F32)).astype(BF16)
    return high, low


def picked(onehot, value, dims=((1,), (0,))):
    high, low = two_parts(value)
    return dot(onehot, high, dims) + dot(onehot, low, dims)


def sigmoid(x):
    return 0.5 * jnp.tanh(0.5 * x) + 0.5


def iota(shape, dim):
    return lax.broadcasted_iota(jnp.int32, shape, dim)


def layer_gradient(looked_up, gain, bias, w_in_ref, w_out_ref, out_grad):
    seq, width = looked_up.shape
    inner = w_out_ref.shape[0]
    mean = jnp.mean(looked_up, axis=1, keepdims=True)
    centered = looked_up - mean
    inv = lax.rsqrt(jnp.mean(centered * centered, axis=1, keepdims=True) + 1e-05)
    xhat = centered * inv
    normed = (xhat * gain + bias).astype(BF16)
    parts, slopes = [], []
    for b in range(4):
        pre = dot(normed, w_in_ref[:, b * inner : (b + 1) * inner])
        sig = sigmoid(pre)
        act = pre * sig
        parts.append(act.astype(BF16))
        slopes.append(sig + act * (1.0 - sig))
    gates, values, queries, keys = parts
    causal = iota((seq, seq), 0) >= iota((seq, seq), 1)
    scale = HEAD ** (-0.5)
    heads = [slice(h * HEAD, (h + 1) * HEAD) for h in range(inner // HEAD)]
    attention, slope_att, mixed = [], [], []
    for h in heads:
        scores = dot(queries[:, h], keys[:, h], ((1,), (1,))) * scale
        sig = sigmoid(scores)
        act = scores * sig
        att = jnp.where(causal, act * (1.0 / seq), 0.0).astype(BF16)
        attention.append(att)
        slope_att.append(jnp.where(causal, (sig + act * (1.0 - sig)) * (scale / seq), 0.0))
        mixed.append(dot(att, values[:, h]))
    mixed = jnp.concatenate(mixed, axis=1)
    mixed = mixed - jnp.mean(mixed, axis=1, keepdims=True)
    inv2 = lax.rsqrt(jnp.mean(mixed * mixed, axis=1, keepdims=True) + 1e-06)
    mhat = mixed * inv2
    d_gated = dot(out_grad, w_out_ref[...], ((1,), (1,))).astype(BF16).astype(F32)
    d_gates = (d_gated * mhat).astype(BF16)
    d_mhat = d_gated * gates.astype(F32)
    d_mixed = inv2 * (
        d_mhat
        - jnp.mean(d_mhat, axis=1, keepdims=True)
        - mhat * jnp.mean(d_mhat * mhat, axis=1, keepdims=True)
    )
    d_mixed = d_mixed.astype(BF16)
    d_values, d_queries, d_keys = [], [], []
    for n, h in enumerate(heads):
        d_att = dot(d_mixed[:, h], values[:, h], ((1,), (1,))).astype(BF16).astype(F32)
        d_values.append(dot(attention[n], d_mixed[:, h], ((0,), (0,))).astype(BF16))
        d_raw = (d_att * slope_att[n]).astype(BF16)
        d_queries.append(dot(d_raw, keys[:, h]).astype(BF16))
        d_keys.append(dot(d_raw, queries[:, h], ((0,), (0,))).astype(BF16))
    d_parts = [
        d_gates,
        jnp.concatenate(d_values, axis=1),
        jnp.concatenate(d_queries, axis=1),
        jnp.concatenate(d_keys, axis=1),
    ]
    d_normed = jnp.zeros((seq, width), F32)
    for b in range(4):
        d_pre = (d_parts[b].astype(F32) * slopes[b]).astype(BF16)
        d_normed = d_normed + dot(d_pre, w_in_ref[:, b * inner : (b + 1) * inner], ((1,), (1,)))
    d_xhat = d_normed.astype(BF16).astype(F32) * gain
    return out_grad.astype(F32) + inv * (
        d_xhat
        - jnp.mean(d_xhat, axis=1, keepdims=True)
        - xhat * jnp.mean(d_xhat * xhat, axis=1, keepdims=True)
    )


def step_kernel(*refs):
    sources, outputs = refs[:INPUTS], refs[INPUTS : INPUTS + 2]
    held = refs[INPUTS + 2 : 2 * INPUTS + 2]
    step_body(sources, *held, *outputs, *refs[2 * INPUTS + 2 :])


def step_body(
    sources,
    slots_ref,
    rows_ref,
    counts_ref,
    hot_ref,
    table_ref,
    gain_ref,
    bias_ref,
    w_in_ref,
    w_out_ref,
    out_grad_ref,
    offsets_ref,
    cold_out,
    hot_out,
    load_sems,
    idx_z,
    idx_n,
    idx_all,
    idx_x,
    send_a,
    recv_a,
    x_send,
    x_recv,
    send_b,
    recv_b,
    hot_s,
    hot_cr,
    hot_xs,
    hot_xr,
    hot_z,
    hot_zr,
    hot_t,
    hot_yr,
    hot_g,
    sems,
    z_s,
    z_r,
    yc_s,
    yc_r,
    xi_s,
    xi_r,
    xh_s,
    xh_r,
    xc_s,
    xc_r,
    hz_s,
    hz_r,
    hy_s,
    hy_r,
    hg_s,
    hg_r,
    xo_s,
    xo_r,
    xp_s,
    xp_r,
):
    z, y, c, x = (lax.axis_index(a) for a in ALL)
    yc = y * NC + c
    me = yc * NZ + z
    width = hot_ref.shape[1]
    lanes = width // NX

    def peers(axis):
        if axis == "yc":
            ways = [o[1:] for o in OFFSETS if o[0] == 0 and o != (0, 0, 0)]
            for oy, oc in ways:
                ty, tc = lax.rem(y + oy, NY), lax.rem(c + oc, NC)
                yield ty * NC + tc, (z, ty, tc, x)
            return
        size = {"z": NZ, "y": NY, "x": NX}[axis]
        for o in sorted(range(1, size), key=lambda o: -hops(o, size)):
            if axis == "z":
                t = lax.rem(z + o, NZ)
                yield t, (t, y, c, x)
            elif axis == "y":
                t = lax.rem(y + o, NY)
                yield t, (z, t, c, x)
            else:
                t = lax.rem(x + o, NX)
                yield t, (z, y, c, t)

    def exchange(axis, src, dst, s, r):
        copies = []
        for n, (t, dev) in enumerate(peers(axis)):
            copies.append(
                pltpu.make_async_remote_copy(
                    src_ref=src(t),
                    dst_ref=dst,
                    send_sem=s.at[n],
                    recv_sem=r.at[n],
                    device_id=dev,
                    device_id_type=MESH,
                )
            )
        for cp in copies:
            cp.start()
        return copies

    def to_sibling(src, dst, n):
        cp = pltpu.make_async_remote_copy(
            src_ref=src,
            dst_ref=dst,
            send_sem=sems.at[n],
            recv_sem=sems.at[n + 1],
            device_id=(z, y, 1 - c, x),
            device_id_type=MESH,
        )
        cp.start()
        return cp

    def arrived(copies):
        for cp in copies:
            cp.wait_recv()

    def tile(q):
        return pl.ds(pl.multiple_of(q * 8, 8), 8)

    def scatter_tiles(src, dst, n, first, last, source):
        for at in range(first, last):
            oz, oy, oc = OFFSETS[at]
            tz, ty, tc = lax.rem(z + oz, NZ), lax.rem(y + oy, NY), lax.rem(c + oc, NC)
            pltpu.make_async_remote_copy(
                src_ref=src.at[tile(source(at, (ty * NC + tc) * NZ + tz))],
                dst_ref=dst.at[tile(me)],
                send_sem=sems.at[n],
                recv_sem=sems.at[n + 1],
                device_id=(tz, ty, tc, x),
                device_id_type=MESH,
            ).start()

    def tiles_wait(ref, n):
        whole = ref.at[pl.ds(0, (OWNERS - 1) * 8)]
        pltpu.make_async_copy(whole, whole, sems.at[n]).wait()

    held = (
        slots_ref,
        rows_ref,
        counts_ref,
        hot_ref,
        table_ref,
        gain_ref,
        bias_ref,
        w_in_ref,
        w_out_ref,
        out_grad_ref,
        offsets_ref,
    )
    loads = [
        pltpu.make_async_copy(src, dst, load_sems.at[n])
        for n, (src, dst) in enumerate(zip(sources, held))
    ]
    barrier = pltpu.get_barrier_semaphore()
    greeted = 0
    for axis in ("z", "yc", "x"):
        for _, dev in peers(axis):
            pl.semaphore_signal(barrier, inc=1, device_id=dev, device_id_type=MESH)
            greeted += 1
    for n in (1, 4, 0, 2, 3, 5, 6, 9, 10, 7, 8):
        loads[n].start()
    loads[1].wait()
    pl.semaphore_wait(barrier, greeted)

    pending = exchange("z", lambda t: rows_ref, idx_z.at[z], z_s, z_r)
    idx_z[z] = rows_ref[...]
    loads[4].wait()
    table_high, table_low = two_parts(table_ref[...])
    arrived(pending)
    every = jnp.concatenate([idx_z[i] for i in range(NZ)], axis=0).astype(F32)
    mine = pltpu.roll(every, lax.rem(8 * 32 - 32 * z, 256), axis=1)[:, :128]
    idx_n[...] = mine
    more = exchange("yc", lambda t: idx_n, idx_all.at[yc], yc_s, yc_r)
    idx_all[yc] = mine
    pending += more
    arrived(more)
    asked = idx_all[...].reshape(OWNERS, 128)
    lane = iota((OWNERS, 128), 1)
    line = iota((OWNERS, table_ref.shape[0]), 1).astype(F32)
    columns = []
    for k in range(2):
        column = jnp.sum(jnp.where(lane == 2 * yc + k, asked, 0.0), axis=1, keepdims=True)
        columns.append(column)
        onehot = (column == line).astype(BF16)
        found = dot(onehot, table_high) + dot(onehot, table_low)
        for i in range(NX):
            send_a[pl.ds(k * NX + i, OWNERS, stride=8), :] = found[:, i * lanes : (i + 1) * lanes]
    scatter_tiles(send_a, recv_a, 0, 0, OWNERS - 1, lambda at, q: q)
    recv_a[tile(me), :] = send_a[tile(me), :]

    both = jnp.where(lane == 0, columns[0], jnp.where(lane == 1, columns[1], 0.0))
    idx_n2 = jnp.transpose(both)[:8, :]
    idx_x[x] = idx_n2
    idx_xs = exchange("x", lambda t: idx_x.at[x], idx_x.at[x], xi_s, xi_r)
    pending += idx_xs

    for n in (0, 2, 3, 5, 6, 9, 10, 7, 8):
        loads[n].wait()
    lane1 = iota((128, 128), 1)
    row1 = iota((128, 128), 0)
    slot_of = jnp.transpose(jnp.broadcast_to(slots_ref[...].astype(F32), (128, 128)))
    counts = jnp.broadcast_to(counts_ref[...].astype(F32), (8, 128)).astype(BF16)
    hot_rows = hot_ref.shape[0]

    def slot_picks(owner):
        live = dot(counts, (row1 == owner).astype(BF16))[:1, :]
        name = (hot_rows + 2 * owner).astype(F32)
        return [((slot_of == name + k) & (live > k)).astype(BF16) for k in range(2)]

    pick_hot = (slot_of == lane1.astype(F32)).astype(BF16)
    picks = slot_picks(lax.rem(lane1, NZ) * NYC + lax.div(lane1, NZ))
    off = offsets_ref[...]
    ahead = (
        lax.rem(z + off[0:1, :], NZ) * NYC
        + lax.rem(y + off[1:2, :], NY) * NC
        + lax.rem(c + off[2:3, :], NC)
    )
    back_picks = slot_picks(jnp.broadcast_to(ahead, (128, 128)))
    looked_hot = picked(pick_hot, hot_ref[...])

    tiles_wait(recv_a, 1)
    looked = []
    for i in range(NX):
        part = looked_hot[:, i * lanes : (i + 1) * lanes]
        for k in range(2):
            part = part + picked(picks[k], recv_a[pl.ds(k * NX + i, OWNERS, stride=8), :])
        looked.append(part)
    looked_up = jnp.concatenate(looked, axis=1)

    d_lookup = layer_gradient(
        looked_up, gain_ref[...], bias_ref[...], w_in_ref, w_out_ref, out_grad_ref[...]
    )

    high, low = two_parts(d_lookup)

    def by_slot(pick):
        return dot(pick, high, ((0,), (0,))) + dot(pick, low, ((0,), (0,)))

    hot_s[...] = by_slot(pick_hot).reshape(2, 64, width)
    swap = to_sibling(hot_s.at[1 - c], hot_cr, 4)
    for k in range(2):
        total = by_slot(back_picks[k])
        for i in range(NX):
            for g in range(GROUPS):
                x_send[i, g, k] = total[g * SPAN : (g + 1) * SPAN, i * lanes : (i + 1) * lanes]
    x_recv[x] = x_send[x]

    def start_cold(g):
        return exchange("x", lambda t: x_send.at[t, g], x_recv.at[x, g], xc_s.at[g], xc_r.at[g])

    cold_x = [start_cold(0)]
    swap.wait()
    for i in range(NX):
        at = slice(i * lanes, (i + 1) * lanes)
        hot_xs[i] = hot_s[c, :, at] + hot_cr[:, at]
    hot_x = exchange("x", lambda t: hot_xs.at[t], hot_xr.at[x], xh_s, xh_r)
    hot_xr[x] = hot_xs[x]
    cold_x += [start_cold(g) for g in range(1, GROUPS)]

    def send_group(g):
        arrived(cold_x[g])
        for p in range(NX):
            for k in range(2):
                send_b[pl.ds(g * SPAN * 8 + p * 2 + k, SPAN, stride=8), :] = x_recv[p, g, k]
        last = min((g + 1) * SPAN, OWNERS - 1)
        scatter_tiles(send_b, recv_b, 2, g * SPAN, last, lambda at, q: at)
        return cold_x[g]

    pending += hot_x
    pending += send_group(0)
    pending += send_group(1)
    arrived(hot_x)
    hot_z[...] = (hot_xr[0] + hot_xr[1] + hot_xr[2] + hot_xr[3]).reshape(NZ, 8, 128)
    hot_zs = exchange("z", lambda t: hot_z.at[t], hot_zr.at[z], hz_s, hz_r)
    hot_zr[z] = hot_z[z]
    pending += send_group(2)
    pending += send_group(3)
    recv_b[tile(me), :] = send_b[tile(OWNERS - 1), :]

    arrived(idx_xs)
    tall = iota((table_ref.shape[0], OWNERS), 0).astype(F32)
    sums = [(tall == idx_x[p, k : k + 1, :]).astype(BF16) for p in range(NX) for k in range(2)]

    arrived(hot_zs)
    hot_t[0] = jnp.sum(hot_zr[...], axis=0)
    hot_ys = exchange("y", lambda t: hot_t.at[0], hot_yr.at[y], hy_s, hy_r)
    hot_yr[y] = hot_t[0]
    arrived(hot_ys)
    hot_t[1] = jnp.sum(hot_yr[...], axis=0)
    hot_gs = exchange("z", lambda t: hot_t.at[1], hot_g.at[z], hg_s, hg_r)
    hot_g[z] = hot_t[1]

    tiles_wait(recv_b, 3)
    grad = jnp.zeros((table_ref.shape[0], 128), F32)
    for n in range(8):
        grad = grad + picked(sums[n], recv_b[pl.ds(n, OWNERS, stride=8), :])
    cold_out[x] = grad
    cold_os = exchange("x", lambda t: cold_out.at[x], cold_out.at[x], xp_s, xp_r)
    arrived(hot_gs)
    hot_out[c, x] = hot_g[...].reshape(64, 128)
    hot_os = exchange("x", lambda t: hot_out.at[c, x], hot_out.at[c, x], xo_s, xo_r)
    arrived(hot_os)
    swap = to_sibling(hot_out.at[c], hot_out.at[c], 6)
    arrived(cold_os)
    swap.wait()
    for cp in pending + hot_zs + hot_ys + hot_gs + cold_os + hot_os:
        cp.wait_send()
    tiles_wait(recv_a, 0)
    tiles_wait(recv_b, 2)


def step(*args):
    hot_table, cold_table = args[3:5]
    vm = pl.BlockSpec(memory_space=pltpu.VMEM)
    dma = pltpu.SemaphoreType.DMA
    cold_rows, width = cold_table.shape
    f32 = lambda *s: pltpu.VMEM(s, F32)
    two = lambda n: [dma((n,)), dma((n,))]
    return pl.pallas_call(
        step_kernel,
        out_shape=(
            jax.ShapeDtypeStruct((NX, cold_rows, width // NX), F32),
            jax.ShapeDtypeStruct((NC, NX, hot_table.shape[0] // NC, width // NX), F32),
        ),
        in_specs=[pl.BlockSpec(memory_space=pltpu.HBM)] * INPUTS,
        out_specs=(vm, vm),
        scratch_shapes=[
            *[pltpu.VMEM(a.shape, a.dtype) for a in args],
            dma((INPUTS,)),
            pltpu.VMEM((NZ, 1, 256), jnp.int32),
            f32(8, 128),
            f32(NYC, 8, 128),
            f32(NX, 8, 128),
            f32(OWNERS * 8, 128),
            f32(OWNERS * 8, 128),
            f32(NX, GROUPS, 2, SPAN, 128),
            f32(NX, GROUPS, 2, SPAN, 128),
            f32(OWNERS * 8, 128),
            f32(OWNERS * 8, 128),
            f32(2, 64, width),
            f32(64, width),
            f32(NX, 64, 128),
            f32(NX, 64, 128),
            f32(NZ, 8, 128),
            f32(NZ, 8, 128),
            f32(2, 8, 128),
            f32(NY, 8, 128),
            f32(NZ, 8, 128),
            dma((8,)),
            *two(NZ),
            *two(NYC),
            *two(NX),
            *two(NX),
            dma((GROUPS, NX)),
            dma((GROUPS, NX)),
            *two(NZ),
            *two(NY),
            *two(NZ),
            *two(NX),
            *two(NX),
        ],
        compiler_params=pltpu.CompilerParams(
            collective_id=0, has_side_effects=True, vmem_limit_bytes=61 << 20
        ),
        cost_estimate=pl.CostEstimate(
            flops=1_500_000_000, bytes_accessed=6_000_000, transcendentals=400_000
        ),
        name="step",
    )(*args)


def update(blocks, table_ref, accum_ref, new_table, new_accum):
    rows, width = table_ref.shape
    lanes = width // NX
    for b in range(rows // 128):
        at = slice(b * 128, (b + 1) * 128)
        grads = blocks(b)
        mean = jnp.sum(sum(g * g for g in grads), axis=1, keepdims=True) * (1.0 / width)
        old = jnp.transpose(jnp.broadcast_to(accum_ref[:, at], (128, 128)))
        new = old + mean
        new_accum[:, at] = jnp.transpose(new)[:1, :]
        rate = STEP_RATE * lax.rsqrt(new)
        for i in range(NX):
            col = slice(i * lanes, (i + 1) * lanes)
            new_table[at, col] = table_ref[at, col] - grads[i] * rate


def adagrad_kernel(
    cold_ref, hot_ref, cold_table, cold_accum, hot_table, hot_accum, o_hot, o_hacc, o_cold, o_cacc
):
    halves = lambda i: jnp.concatenate([hot_ref[0, i], hot_ref[1, i]], axis=0)
    update(lambda b: [halves(i) for i in range(NX)], hot_table, hot_accum, o_hot, o_hacc)
    cold = lambda b: [cold_ref[i, b * 128 : (b + 1) * 128, :] for i in range(NX)]
    update(cold, cold_table, cold_accum, o_cold, o_cacc)


def adagrad(cold_grad, hot_grad, cold_table, cold_accum, hot_table, hot_accum):
    vm = pl.BlockSpec(memory_space=pltpu.VMEM)
    cold_accum, hot_accum = cold_accum.reshape(1, -1), hot_accum.reshape(1, -1)
    out = pl.pallas_call(
        adagrad_kernel,
        out_shape=tuple(
            jax.ShapeDtypeStruct(a.shape, F32)
            for a in (hot_table, hot_accum, cold_table, cold_accum)
        ),
        in_specs=[vm] * 6,
        out_specs=(vm,) * 4,
        compiler_params=pltpu.CompilerParams(vmem_limit_bytes=16 << 20),
        name="adagrad",
    )(cold_grad, hot_grad, cold_table, cold_accum, hot_table, hot_accum)
    return out[0], out[1].reshape(-1), out[2], out[3].reshape(-1)


def on_device(
    event_slots,
    fetch_rows,
    fetch_counts,
    hot_table,
    hot_accum,
    cold_table,
    cold_accum,
    ln_gain,
    ln_bias,
    w_in,
    w_out,
    out_grad,
):
    cold_grad, hot_grad = step(
        event_slots,
        fetch_rows,
        fetch_counts,
        hot_table,
        cold_table,
        ln_gain.reshape(1, -1),
        ln_bias.reshape(1, -1),
        w_in,
        w_out,
        out_grad,
        jnp.asarray(np.array(OFFSETS, np.int32).T),
    )
    return adagrad(cold_grad, hot_grad, cold_table, cold_accum, hot_table, hot_accum)


def solution(mesh):
    finer = Mesh(mesh.devices.reshape(NZ, NY, NC, NX), ALL)
    return jax.shard_map(
        on_device,
        mesh=finer,
        in_specs=(
            P(ALL, None),
            P(ALL, None),
            P(ALL, None),
            P(),
            P(),
            P(BY_ROWS, None),
            P(BY_ROWS),
            P(),
            P(),
            P(),
            P(),
            P(ALL, None),
        ),
        out_specs=(P(), P(), P(BY_ROWS, None), P(BY_ROWS)),
        check_vma=False,
    )
```

```python
import functools

import jax
import jax.numpy as jnp
import numpy as np
from jax import lax
from jax.experimental import pallas as pl
from jax.experimental.pallas import tpu as pltpu
from jax.sharding import Mesh
from jax.sharding import PartitionSpec as P

HEAD = 128
STEP_RATE = 0.5
NZ, NY, NC, NX = 8, 8, 2, 4
NYC = NY * NC
OWNERS = NZ * NYC
INPUTS = 11
GROUPS = 4
SPAN = OWNERS // GROUPS


def hops(offset, size):
    return min(offset, size - offset)


def farthest_first():
    offsets = [(a, b, k) for a in range(NZ) for b in range(NY) for k in range(NC)]
    mixed = [offsets[n * 37 % OWNERS] for n in range(OWNERS)]
    far = lambda o: max(hops(o[0], NZ), hops(o[1], NY))
    both = lambda o: hops(o[0], NZ) + hops(o[1], NY)
    return sorted(mixed, key=lambda o: (-far(o), -both(o), o == (0, 0, 0)))


OFFSETS = farthest_first()
ALL = ("z", "y", "c", "x")
BY_ROWS = ("z", "y", "c")
MESH = pl.DeviceIdType.MESH
F32, BF16 = jnp.float32, jnp.bfloat16


def dot(a, b, dims=((1,), (0,))):
    return lax.dot_general(a, b, (dims, ((), ())), preferred_element_type=F32)


def two_parts(value):
    high = value.astype(BF16)
    low = (value - high.astype(F32)).astype(BF16)
    return high, low


def picked(onehot, value, dims=((1,), (0,))):
    high, low = two_parts(value)
    return dot(onehot, high, dims) + dot(onehot, low, dims)


def sigmoid(x):
    return 0.5 * jnp.tanh(0.5 * x) + 0.5


def iota(shape, dim):
    return lax.broadcasted_iota(jnp.int32, shape, dim)


def layer_gradient(looked_up, gain, bias, w_in_ref, d_gated, out_grad):
    seq, width = looked_up.shape
    inner = d_gated.shape[1]
    mean = jnp.mean(looked_up, axis=1, keepdims=True)
    centered = looked_up - mean
    inv = lax.rsqrt(jnp.mean(centered * centered, axis=1, keepdims=True) + 1e-05)
    xhat = centered * inv
    normed = (xhat * gain + bias).astype(BF16)
    parts, slopes = [], []
    for b in range(4):
        pre = dot(normed, w_in_ref[:, b * inner : (b + 1) * inner])
        sig = sigmoid(pre)
        act = pre * sig
        parts.append(act.astype(BF16))
        slopes.append(sig + act * (1.0 - sig))
    gates, values, queries, keys = parts
    causal = iota((seq, seq), 0) >= iota((seq, seq), 1)
    scale = HEAD ** (-0.5)
    heads = [slice(h * HEAD, (h + 1) * HEAD) for h in range(inner // HEAD)]
    attention, slope_att, mixed = [], [], []
    for h in heads:
        scores = dot(queries[:, h], keys[:, h], ((1,), (1,))) * scale
        sig = sigmoid(scores)
        act = scores * sig
        att = jnp.where(causal, act * (1.0 / seq), 0.0).astype(BF16)
        attention.append(att)
        slope_att.append(jnp.where(causal, (sig + act * (1.0 - sig)) * (scale / seq), 0.0))
        mixed.append(dot(att, values[:, h]))
    mixed = jnp.concatenate(mixed, axis=1)
    mixed = mixed - jnp.mean(mixed, axis=1, keepdims=True)
    inv2 = lax.rsqrt(jnp.mean(mixed * mixed, axis=1, keepdims=True) + 1e-06)
    mhat = mixed * inv2
    d_gates = (d_gated * mhat).astype(BF16)
    d_mhat = d_gated * gates.astype(F32)
    d_mixed = inv2 * (
        d_mhat
        - jnp.mean(d_mhat, axis=1, keepdims=True)
        - mhat * jnp.mean(d_mhat * mhat, axis=1, keepdims=True)
    )
    d_mixed = d_mixed.astype(BF16)
    d_values, d_queries, d_keys = [], [], []
    for n, h in enumerate(heads):
        d_att = dot(d_mixed[:, h], values[:, h], ((1,), (1,))).astype(BF16).astype(F32)
        d_values.append(dot(attention[n], d_mixed[:, h], ((0,), (0,))).astype(BF16))
        d_raw = (d_att * slope_att[n]).astype(BF16)
        d_queries.append(dot(d_raw, keys[:, h]).astype(BF16))
        d_keys.append(dot(d_raw, queries[:, h], ((0,), (0,))).astype(BF16))
    d_parts = [
        d_gates,
        jnp.concatenate(d_values, axis=1),
        jnp.concatenate(d_queries, axis=1),
        jnp.concatenate(d_keys, axis=1),
    ]
    d_normed = jnp.zeros((seq, width), F32)
    for b in range(4):
        d_pre = (d_parts[b].astype(F32) * slopes[b]).astype(BF16)
        d_normed = d_normed + dot(d_pre, w_in_ref[:, b * inner : (b + 1) * inner], ((1,), (1,)))
    d_xhat = d_normed.astype(BF16).astype(F32) * gain
    return out_grad.astype(F32) + inv * (
        d_xhat
        - jnp.mean(d_xhat, axis=1, keepdims=True)
        - xhat * jnp.mean(d_xhat * xhat, axis=1, keepdims=True)
    )


def step_kernel(*refs):
    sources, outputs = refs[:INPUTS], refs[INPUTS : INPUTS + 2]
    held = refs[INPUTS + 2 : 2 * INPUTS + 2]
    step_body(sources, *held, *outputs, *refs[2 * INPUTS + 2 :])


def step_body(
    sources,
    slots_ref,
    rows_ref,
    counts_ref,
    hot_ref,
    table_ref,
    gain_ref,
    bias_ref,
    w_in_ref,
    w_out_ref,
    out_grad_ref,
    offsets_ref,
    cold_out,
    hot_out,
    load_sems,
    idx_z,
    idx_n,
    idx_all,
    idx_x,
    send_a,
    recv_a,
    x_send,
    x_recv,
    send_b,
    recv_b,
    hot_s,
    hot_cr,
    hot_z,
    hot_zr,
    hot_t,
    hot_yr,
    hot_t2,
    sems,
    z_s,
    z_r,
    yc_s,
    yc_r,
    xi_s,
    xi_r,
    xc_s,
    xc_r,
    hz_s,
    hz_r,
    hy_s,
    hy_r,
    hg_s,
    hg_r,
    xp_s,
    xp_r,
):
    z, y, c, x = (lax.axis_index(a) for a in ALL)
    yc = y * NC + c
    me = yc * NZ + z
    width = hot_ref.shape[1]
    lanes = width // NX

    def peers(axis):
        if axis == "yc":
            ways = [o[1:] for o in OFFSETS if o[0] == 0 and o != (0, 0, 0)]
            for oy, oc in ways:
                ty, tc = lax.rem(y + oy, NY), lax.rem(c + oc, NC)
                yield ty * NC + tc, (z, ty, tc, x)
            return
        if axis == "zx":
            ways = [(a, b) for a in range(NZ) for b in range(NX) if (a, b) != (0, 0)]
            for oz, ox in sorted(ways, key=lambda o: -hops(o[0], NZ) - hops(o[1], NX)):
                tz, tx = lax.rem(z + oz, NZ), lax.rem(x + ox, NX)
                yield (tz, tx), (tz, y, c, tx)
            return
        size = {"z": NZ, "y": NY, "x": NX}[axis]
        for o in sorted(range(1, size), key=lambda o: -hops(o, size)):
            if axis == "z":
                t = lax.rem(z + o, NZ)
                yield t, (t, y, c, x)
            elif axis == "y":
                t = lax.rem(y + o, NY)
                yield t, (z, t, c, x)
            else:
                t = lax.rem(x + o, NX)
                yield t, (z, y, c, t)

    def exchange(axis, src, dst, s, r):
        copies = []
        for n, (t, dev) in enumerate(peers(axis)):
            copies.append(
                pltpu.make_async_remote_copy(
                    src_ref=src(t),
                    dst_ref=dst,
                    send_sem=s.at[n],
                    recv_sem=r.at[n],
                    device_id=dev,
                    device_id_type=MESH,
                )
            )
        for cp in copies:
            cp.start()
        return copies

    def to_sibling(src, dst, n):
        cp = pltpu.make_async_remote_copy(
            src_ref=src,
            dst_ref=dst,
            send_sem=sems.at[n],
            recv_sem=sems.at[n + 1],
            device_id=(z, y, 1 - c, x),
            device_id_type=MESH,
        )
        cp.start()
        return cp

    def arrived(copies):
        for cp in copies:
            cp.wait_recv()

    def tile(q):
        return pl.ds(pl.multiple_of(q * 8, 8), 8)

    def scatter_tiles(src, dst, n, first, last, source):
        for at in range(first, last):
            oz, oy, oc = OFFSETS[at]
            tz, ty, tc = lax.rem(z + oz, NZ), lax.rem(y + oy, NY), lax.rem(c + oc, NC)
            pltpu.make_async_remote_copy(
                src_ref=src.at[tile(source(at, (ty * NC + tc) * NZ + tz))],
                dst_ref=dst.at[tile(me)],
                send_sem=sems.at[n],
                recv_sem=sems.at[n + 1],
                device_id=(tz, ty, tc, x),
                device_id_type=MESH,
            ).start()

    def tiles_wait(ref, n):
        whole = ref.at[pl.ds(0, (OWNERS - 1) * 8)]
        pltpu.make_async_copy(whole, whole, sems.at[n]).wait()

    held = (
        slots_ref,
        rows_ref,
        counts_ref,
        hot_ref,
        table_ref,
        gain_ref,
        bias_ref,
        w_in_ref,
        w_out_ref,
        out_grad_ref,
        offsets_ref,
    )
    loads = [
        pltpu.make_async_copy(src, dst, load_sems.at[n])
        for n, (src, dst) in enumerate(zip(sources, held))
    ]
    barrier = pltpu.get_barrier_semaphore()
    greeted = 0
    for axis in ("z", "yc", "x"):
        for _, dev in peers(axis):
            pl.semaphore_signal(barrier, inc=1, device_id=dev, device_id_type=MESH)
            greeted += 1
    for n in (1, 4, 0, 2, 3, 5, 6, 9, 10, 7, 8):
        loads[n].start()
    loads[1].wait()
    pl.semaphore_wait(barrier, greeted)

    pending = exchange("z", lambda t: rows_ref, idx_z.at[z], z_s, z_r)
    idx_z[z] = rows_ref[...]
    loads[4].wait()
    table_high, table_low = two_parts(table_ref[...])
    arrived(pending)
    every = jnp.concatenate([idx_z[i] for i in range(NZ)], axis=0).astype(F32)
    mine = pltpu.roll(every, lax.rem(8 * 32 - 32 * z, 256), axis=1)[:, :128]
    idx_n[...] = mine
    more = exchange("yc", lambda t: idx_n, idx_all.at[yc], yc_s, yc_r)
    idx_all[yc] = mine
    pending += more
    arrived(more)
    asked = idx_all[...].reshape(OWNERS, 128)
    lane = iota((OWNERS, 128), 1)
    line = iota((OWNERS, table_ref.shape[0]), 1).astype(F32)
    columns = []
    for k in range(2):
        column = jnp.sum(jnp.where(lane == 2 * yc + k, asked, 0.0), axis=1, keepdims=True)
        columns.append(column)
        onehot = (column == line).astype(BF16)
        found = dot(onehot, table_high) + dot(onehot, table_low)
        for i in range(NX):
            send_a[pl.ds(k * NX + i, OWNERS, stride=8), :] = found[:, i * lanes : (i + 1) * lanes]
    scatter_tiles(send_a, recv_a, 0, 0, OWNERS - 1, lambda at, q: q)
    recv_a[tile(me), :] = send_a[tile(me), :]

    both = jnp.where(lane == 0, columns[0], jnp.where(lane == 1, columns[1], 0.0))
    idx_n2 = jnp.transpose(both)[:8, :]
    idx_x[x] = idx_n2
    idx_xs = exchange("x", lambda t: idx_x.at[x], idx_x.at[x], xi_s, xi_r)
    pending += idx_xs

    for n in (0, 2, 3, 5, 6, 9, 10, 7, 8):
        loads[n].wait()
    lane1 = iota((128, 128), 1)
    row1 = iota((128, 128), 0)
    slot_of = jnp.transpose(jnp.broadcast_to(slots_ref[...].astype(F32), (128, 128)))
    counts = jnp.broadcast_to(counts_ref[...].astype(F32), (8, 128)).astype(BF16)
    hot_rows = hot_ref.shape[0]

    def slot_picks(owner):
        live = dot(counts, (row1 == owner).astype(BF16))[:1, :]
        name = (hot_rows + 2 * owner).astype(F32)
        return [((slot_of == name + k) & (live > k)).astype(BF16) for k in range(2)]

    pick_hot = (slot_of == lane1.astype(F32)).astype(BF16)
    picks = slot_picks(lax.rem(lane1, NZ) * NYC + lax.div(lane1, NZ))
    off = offsets_ref[...]
    ahead = (
        lax.rem(z + off[0:1, :], NZ) * NYC
        + lax.rem(y + off[1:2, :], NY) * NC
        + lax.rem(c + off[2:3, :], NC)
    )
    back_picks = slot_picks(jnp.broadcast_to(ahead, (128, 128)))
    looked_hot = picked(pick_hot, hot_ref[...])
    d_gated = dot(out_grad_ref[...], w_out_ref[...], ((1,), (1,))).astype(BF16).astype(F32)

    arrived(idx_xs)
    tiles_wait(recv_a, 1)
    looked = []
    for i in range(NX):
        part = looked_hot[:, i * lanes : (i + 1) * lanes]
        for k in range(2):
            part = part + picked(picks[k], recv_a[pl.ds(k * NX + i, OWNERS, stride=8), :])
        looked.append(part)
    looked_up = jnp.concatenate(looked, axis=1)

    d_lookup = layer_gradient(
        looked_up, gain_ref[...], bias_ref[...], w_in_ref, d_gated, out_grad_ref[...]
    )

    high, low = two_parts(d_lookup)

    def by_slot(pick):
        return dot(pick, high, ((0,), (0,))) + dot(pick, low, ((0,), (0,)))

    hot_s[...] = by_slot(pick_hot).reshape(2, 64, width)
    swap = to_sibling(hot_s.at[1 - c], hot_cr, 4)
    for k in range(2):
        total = by_slot(back_picks[k])
        for i in range(NX):
            for g in range(GROUPS):
                x_send[i, g, k] = total[g * SPAN : (g + 1) * SPAN, i * lanes : (i + 1) * lanes]
    x_recv[x] = x_send[x]

    def start_cold(g):
        return exchange("x", lambda t: x_send.at[t, g], x_recv.at[x, g], xc_s.at[g], xc_r.at[g])

    cold_x = [start_cold(0)]
    swap.wait()
    own = (hot_s[c] + hot_cr[...]).reshape(NZ, 8, width)
    for i in range(NX):
        hot_z[:, i] = own[:, :, i * lanes : (i + 1) * lanes]
    hot_zs = exchange("zx", lambda t: hot_z.at[t[0], t[1]], hot_zr.at[z, x], hz_s, hz_r)
    hot_zr[z, x] = hot_z[z, x]
    cold_x += [start_cold(g) for g in range(1, GROUPS)]

    def send_group(g):
        arrived(cold_x[g])
        for p in range(NX):
            for k in range(2):
                send_b[pl.ds(g * SPAN * 8 + p * 2 + k, SPAN, stride=8), :] = x_recv[p, g, k]
        last = min((g + 1) * SPAN, OWNERS - 1)
        scatter_tiles(send_b, recv_b, 2, g * SPAN, last, lambda at, q: at)
        return cold_x[g]

    pending += send_group(0)
    pending += send_group(1)
    pending += send_group(2)
    arrived(hot_zs)
    hot_t[...] = jnp.sum(hot_zr[...].reshape(NZ * NX, 8, 128), axis=0)
    hot_ys = exchange("y", lambda t: hot_t, hot_yr.at[y], hy_s, hy_r)
    hot_yr[y] = hot_t[...]
    pending += send_group(3)
    recv_b[tile(me), :] = send_b[tile(OWNERS - 1), :]

    tall = iota((table_ref.shape[0], OWNERS), 0).astype(F32)
    sums = [(tall == idx_x[p, k : k + 1, :]).astype(BF16) for p in range(NX) for k in range(2)]

    arrived(hot_ys)
    hot_t2[...] = jnp.sum(hot_yr[...], axis=0)
    hot_gs = exchange("zx", lambda t: hot_t2, hot_out.at[c, z, x], hg_s, hg_r)
    hot_out[c, z, x] = hot_t2[...]

    tiles_wait(recv_b, 3)
    grad = jnp.zeros((table_ref.shape[0], 128), F32)
    for n in range(8):
        grad = grad + picked(sums[n], recv_b[pl.ds(n, OWNERS, stride=8), :])
    cold_out[x] = grad
    cold_os = exchange("x", lambda t: cold_out.at[x], cold_out.at[x], xp_s, xp_r)
    arrived(hot_gs)
    swap = to_sibling(hot_out.at[c], hot_out.at[c], 6)
    arrived(cold_os)
    swap.wait()
    for cp in pending + hot_zs + hot_ys + hot_gs + cold_os:
        cp.wait_send()
    tiles_wait(recv_a, 0)
    tiles_wait(recv_b, 2)


def step(*args):
    hot_table, cold_table = args[3:5]
    vm = pl.BlockSpec(memory_space=pltpu.VMEM)
    dma = pltpu.SemaphoreType.DMA
    cold_rows, width = cold_table.shape
    f32 = lambda *s: pltpu.VMEM(s, F32)
    two = lambda n: [dma((n,)), dma((n,))]
    return pl.pallas_call(
        step_kernel,
        out_shape=(
            pltpu.VMEM((NX, cold_rows, width // NX), F32),
            pltpu.VMEM((NC, NZ, NX, hot_table.shape[0] // (NC * NZ), width // NX), F32),
        ),
        in_specs=[pl.BlockSpec(memory_space=pltpu.HBM)] * INPUTS,
        out_specs=(vm, vm),
        scratch_shapes=[
            *[pltpu.VMEM(a.shape, a.dtype) for a in args],
            dma((INPUTS,)),
            pltpu.VMEM((NZ, 1, 256), jnp.int32),
            f32(8, 128),
            f32(NYC, 8, 128),
            f32(NX, 8, 128),
            f32(OWNERS * 8, 128),
            f32(OWNERS * 8, 128),
            f32(NX, GROUPS, 2, SPAN, 128),
            f32(NX, GROUPS, 2, SPAN, 128),
            f32(OWNERS * 8, 128),
            f32(OWNERS * 8, 128),
            f32(2, 64, width),
            f32(64, width),
            f32(NZ, NX, 8, 128),
            f32(NZ, NX, 8, 128),
            f32(8, 128),
            f32(NY, 8, 128),
            f32(8, 128),
            dma((8,)),
            *two(NZ),
            *two(NYC),
            *two(NX),
            dma((GROUPS, NX)),
            dma((GROUPS, NX)),
            *two(NZ * NX),
            *two(NY),
            *two(NZ * NX),
            *two(NX),
        ],
        compiler_params=pltpu.CompilerParams(
            collective_id=0, has_side_effects=True, vmem_limit_bytes=61 << 20
        ),
        cost_estimate=pl.CostEstimate(
            flops=1_500_000_000, bytes_accessed=6_000_000, transcendentals=400_000
        ),
        name="step",
    )(*args)


def update(blocks, table_ref, accum_ref, new_table, new_accum):
    rows, width = table_ref.shape
    lanes = width // NX
    for b in range(rows // 128):
        at = slice(b * 128, (b + 1) * 128)
        grads = blocks(b)
        mean = jnp.sum(sum(g * g for g in grads), axis=1, keepdims=True) * (1.0 / width)
        old = jnp.transpose(jnp.broadcast_to(accum_ref[:, at], (128, 128)))
        new = old + mean
        new_accum[:, at] = jnp.transpose(new)[:1, :]
        rate = STEP_RATE * lax.rsqrt(new)
        for i in range(NX):
            col = slice(i * lanes, (i + 1) * lanes)
            new_table[at, col] = table_ref[at, col] - grads[i] * rate


def adagrad_kernel(
    cold_ref, hot_ref, cold_table, cold_accum, hot_table, hot_accum, o_hot, o_hacc, o_cold, o_cacc
):
    hot = lambda i: hot_ref[:, :, i].reshape(128, 128)
    update(lambda b: [hot(i) for i in range(NX)], hot_table, hot_accum, o_hot, o_hacc)
    cold = lambda b: [cold_ref[i, b * 128 : (b + 1) * 128, :] for i in range(NX)]
    update(cold, cold_table, cold_accum, o_cold, o_cacc)


def adagrad(cold_grad, hot_grad, cold_table, cold_accum, hot_table, hot_accum):
    vm = pl.BlockSpec(memory_space=pltpu.VMEM)
    cold_accum, hot_accum = cold_accum.reshape(1, -1), hot_accum.reshape(1, -1)
    out = pl.pallas_call(
        adagrad_kernel,
        out_shape=tuple(
            jax.ShapeDtypeStruct(a.shape, F32)
            for a in (hot_table, hot_accum, cold_table, cold_accum)
        ),
        in_specs=[vm] * 6,
        out_specs=(vm,) * 4,
        compiler_params=pltpu.CompilerParams(vmem_limit_bytes=16 << 20),
        name="adagrad",
    )(cold_grad, hot_grad, cold_table, cold_accum, hot_table, hot_accum)
    return out[0], out[1].reshape(-1), out[2], out[3].reshape(-1)


def on_device(
    event_slots,
    fetch_rows,
    fetch_counts,
    hot_table,
    hot_accum,
    cold_table,
    cold_accum,
    ln_gain,
    ln_bias,
    w_in,
    w_out,
    out_grad,
):
    cold_grad, hot_grad = step(
        event_slots,
        fetch_rows,
        fetch_counts,
        hot_table,
        cold_table,
        ln_gain.reshape(1, -1),
        ln_bias.reshape(1, -1),
        w_in,
        w_out,
        out_grad,
        jnp.asarray(np.array(OFFSETS, np.int32).T),
    )
    return adagrad(cold_grad, hot_grad, cold_table, cold_accum, hot_table, hot_accum)


def solution(mesh):
    finer = Mesh(mesh.devices.reshape(NZ, NY, NC, NX), ALL)
    return jax.shard_map(
        on_device,
        mesh=finer,
        in_specs=(
            P(ALL, None),
            P(ALL, None),
            P(ALL, None),
            P(),
            P(),
            P(BY_ROWS, None),
            P(BY_ROWS),
            P(),
            P(),
            P(),
            P(),
            P(ALL, None),
        ),
        out_specs=(P(), P(), P(BY_ROWS, None), P(BY_ROWS)),
        check_vma=False,
    )
```
